512 devices in a mesh: req: 32 (over x_hi, z), pre: 16 (over x_lo, y, core).
Axes of the slice: x: 4 (x_hi: 2, x_lo: 2; x = x_hi * 2 + x_lo), y: 4, z: 16, core: 2. Of those that a mesh axis runs over, the one named last changes fastest.
Arguments:
- queries: bfloat16 [128, 128, 576], P('req', 'pre'), may hold values from -120 to 120
- root_latent: bfloat16 [65536, 576], P('pre'), may hold values from -40 to 40
- suffix_latent: bfloat16 [128, 4096, 576], P('req', 'pre'), may hold values from -40 to 40
- suffix_length: int32 [128], P('req'), may hold values from 1 to 4096
- branch_pick: int32 [128], P('req'), may hold values from 0 to 3
Outputs:
- attended: bfloat16 [128, 128, 512], P('req', 'pre')
The draws below stay inside these ranges and needn't reach their ends.
All inputs are finite; a program needn't handle non-finite values.
Results may differ from the reference program's by a relative error of at most 0.015.
Values may be sent and summed in bfloat16 or wider, within the bound.
A program may use at most 128 MiB of HBM per device.

```python
import math
import jax
import jax.numpy as jnp
from jax import lax

HEADS = 128
LATENT = 512
REQ_DEV = 4
BR_DEV = 4
SUF = 4096
KV = 576
REQ = 128
ROOT = 65536
BRANCHES = 128


def spread_row(key, index, low, high):
    row_key = jax.random.fold_in(key, index)
    first, second = jax.random.split(row_key)
    base = jax.random.truncated_normal(first, -6.0, 6.0, (KV,), jnp.float32)
    level = jnp.exp(jax.random.uniform(second, (), jnp.float32, math.log(low), math.log(high)))
    return (jnp.clip(base * level, -40.0, 40.0), level)


def root_rows(key, indices, low, high):
    root_key = jax.random.fold_in(key, 11)
    return jax.vmap(lambda index: spread_row(root_key, index, low, high))(indices)


def suffix_rows(key, indices, low, high):
    suffix_key = jax.random.fold_in(key, 13)
    return jax.vmap(lambda index: spread_row(suffix_key, index, low, high))(indices)


def branch_lengths(key):
    key = jax.random.fold_in(key, 5)
    first, second, third = jax.random.split(key, 3)
    values = jax.random.randint(first, (BRANCHES,), 1, SUF + 1)
    full_one = jax.random.randint(second, (), 0, BRANCHES)
    short_one = (full_one + 1 + jax.random.randint(third, (), 0, BRANCHES - 1)) % BRANCHES
    places = jnp.arange(BRANCHES)
    values = jnp.where(places == full_one, SUF, values)
    values = jnp.where(places == short_one, 1, values)
    return values.astype(jnp.int32)


def branch_choice(key):
    key = jax.random.fold_in(key, 7)
    first, second, third = jax.random.split(key, 3)
    picks = jax.random.randint(first, (REQ,), 0, BR_DEV)
    high_one = jax.random.randint(second, (), 0, REQ)
    low_one = (high_one + 1 + jax.random.randint(third, (), 0, REQ - 1)) % REQ
    places = jnp.arange(REQ)
    picks = jnp.where(places == high_one, BR_DEV - 1, picks)
    picks = jnp.where(places == low_one, 0, picks)
    return picks.astype(jnp.int32)


def draw_root_latent(key, part):
    rows, levels = root_rows(key, jnp.arange(ROOT), 0.5, 4.0)
    return rows.astype(jnp.bfloat16)


def draw_suffix_latent(key, part):
    rows, levels = suffix_rows(key, jnp.arange(BRANCHES * SUF), 0.5, 4.0)
    return rows.reshape(BRANCHES, SUF, KV).astype(jnp.bfloat16)


def draw_suffix_length(key, part):
    return branch_lengths(key)


def draw_branch_pick(key, part):
    return branch_choice(key)


def draw_queries(key, part):
    base_key = key
    key = jax.random.fold_in(key, 2)
    keys = jax.random.split(key, 5)
    base = jax.random.truncated_normal(keys[0], -6.0, 6.0, (REQ, HEADS, KV), jnp.float32)
    low, high = (0.5, 4.0)
    lengths = branch_lengths(base_key)
    picks = branch_choice(base_key)
    branch = jnp.arange(REQ) // REQ_DEV * BR_DEV + picks
    length = lengths[branch][:, None]
    inside = jax.random.randint(keys[1], (REQ, HEADS), 0, length)
    outside = jax.random.randint(keys[2], (REQ, HEADS), jnp.minimum(length, SUF - 1), SUF)
    kinds = jax.random.randint(keys[3], (REQ, HEADS), 0, 16)
    position = jnp.where(kinds == 1, outside, inside)
    flat = (branch[:, None] * SUF + position).reshape(-1)
    rows, levels = suffix_rows(base_key, flat, low, high)
    rows = rows.astype(jnp.bfloat16).astype(jnp.float32)
    direction = (rows / levels[:, None]).reshape(REQ, HEADS, KV)
    strength = jax.random.uniform(keys[4], (REQ, HEADS, 1), jnp.float32, 0.5, 1.5)
    result = jnp.where((kinds <= 1)[:, :, None], base + strength * direction, base)
    return jnp.clip(result, -120.0, 120.0).astype(jnp.bfloat16)


def setup_inputs(seed: int = 0) -> dict:
    streams_of = jax.random.split(jax.random.key(seed), 6)
    return {
        "queries": draw_queries(jax.random.fold_in(streams_of[5], 71), 0),
        "root_latent": draw_root_latent(jax.random.fold_in(streams_of[5], 71), 0),
        "suffix_latent": draw_suffix_latent(jax.random.fold_in(streams_of[5], 71), 0),
        "suffix_length": draw_suffix_length(jax.random.fold_in(streams_of[5], 71), 0),
        "branch_pick": draw_branch_pick(jax.random.fold_in(streams_of[5], 71), 0),
    }


score_scale = 192.0 ** -0.5


def reference(queries, root_latent, suffix_latent, suffix_length, branch_pick):
    root_values = root_latent[:, :LATENT]

    def single(index):
        query = queries[index]
        branch = (index // REQ_DEV) * BR_DEV + branch_pick[index]
        branch = branch.astype(jnp.int32)
        suffix = lax.dynamic_index_in_dim(suffix_latent, branch, 0, keepdims=False)
        length = lax.dynamic_index_in_dim(suffix_length, branch, 0, keepdims=False)
        root_scores = jnp.dot(query, root_latent.T, preferred_element_type=jnp.float32) * score_scale
        suffix_scores = jnp.dot(query, suffix.T, preferred_element_type=jnp.float32) * score_scale
        valid = jnp.arange(SUF, dtype=jnp.int32)[None, :] < length
        suffix_scores = jnp.where(valid, suffix_scores, -jnp.inf)
        top = jnp.maximum(jnp.max(root_scores, axis=1), jnp.max(suffix_scores, axis=1))
        root_weights = jnp.exp(root_scores - top[:, None])
        suffix_weights = jnp.where(valid, jnp.exp(suffix_scores - top[:, None]), 0.0)
        total = jnp.sum(root_weights, axis=1) + jnp.sum(suffix_weights, axis=1)
        numerator = jnp.dot(root_weights.astype(jnp.bfloat16), root_values, preferred_element_type=jnp.float32)
        numerator = numerator + jnp.dot(suffix_weights.astype(jnp.bfloat16), suffix[:, :LATENT], preferred_element_type=jnp.float32)
        return (numerator / total[:, None]).astype(jnp.bfloat16)

    return lax.map(single, jnp.arange(REQ, dtype=jnp.int32))
```

```python
import functools

import jax
import jax.numpy as jnp
from jax import lax
from jax.experimental import pallas as pl
from jax.experimental.pallas import tpu as pltpu
from jax.sharding import PartitionSpec as P

MESH = pl.DeviceIdType.MESH
LATENT = 512
SCORE_SCALE = 192.0 ** (-0.5)
EXP2_SCALE = SCORE_SCALE * 1.4426950408889634
YS, XS = 4, 2
CHIPS = XS * YS
PEERS = [(dx, dy) for dx in range(XS) for dy in range(YS) if (dx, dy) != (0, 0)]
BLOCK = 512
ROOT_PARTS = 4


def kernel(
    q_hbm,
    root_hbm,
    suffix_hbm,
    lengths,
    picks,
    o_ref,
    root,
    suffix,
    near,
    far,
    scores,
    suffix_scores,
    pair_out,
    pair_top,
    pair_sum,
    got_out,
    got_top,
    got_sum,
    part_out,
    part_stat,
    all_out,
    all_stat,
    load_sem,
    ask_send,
    ask_recv,
    fwd_send,
    fwd_recv,
    pair_send,
    pair_recv,
    out_send,
    out_recv,
    stat_send,
    stat_recv,
):
    me = lax.axis_index("pre")
    core = me % 2
    chip = me // 2
    x, y = chip // YS, chip % YS
    sibling = me + 1 - 2 * core
    reqs = lengths.shape[0]
    rows = q_hbm.shape[0]
    heads = rows // reqs
    many = CHIPS * rows
    positions = root_hbm.shape[1]
    tail = suffix_hbm.shape[2]

    def target(peer):
        dx, dy = peer
        return (((x + dx) % XS) * YS + (y + dy) % YS) * 2 + core

    def source_chip(peer):
        dx, dy = peer
        return ((x + dx) % XS) * YS + (y + YS - dy) % YS

    barrier = pltpu.get_barrier_semaphore()
    for peer in PEERS:
        pl.semaphore_signal(barrier, inc=1, device_id={"pre": target(peer)}, device_id_type=MESH)
    pl.semaphore_signal(barrier, inc=1, device_id={"pre": sibling}, device_id_type=MESH)

    own = pltpu.make_async_copy(q_hbm, near.at[chip], load_sem.at[0])
    own.start()
    depth = root_hbm.shape[0] // ROOT_PARTS
    loads = [
        pltpu.make_async_copy(
            root_hbm.at[pl.ds(i * depth, depth)], root.at[pl.ds(i * depth, depth)], load_sem.at[2 + i]
        )
        for i in range(ROOT_PARTS)
    ]
    loads.append(pltpu.make_async_copy(suffix_hbm, suffix, load_sem.at[1]))
    for load in loads:
        load.start()
    own.wait()
    pl.semaphore_wait(barrier, len(PEERS) + 1)

    def remote(src, dst, send, recv, device):
        return pltpu.make_async_remote_copy(
            src_ref=src,
            dst_ref=dst,
            send_sem=send,
            recv_sem=recv,
            device_id={"pre": device},
            device_id_type=MESH,
        )

    asks = [
        remote(near.at[chip], near.at[chip], ask_send.at[i], ask_recv.at[i], target(peer))
        for i, peer in enumerate(PEERS)
    ]
    for ask in asks:
        ask.start()
    passes = [remote(near.at[chip], far.at[chip], fwd_send.at[7], fwd_recv.at[7], sibling)]
    passes[0].start()
    for load in loads:
        load.wait()
    for i, peer in enumerate(PEERS):
        asks[i].wait_recv()
        held = source_chip(peer)
        forward = remote(near.at[held], far.at[held], fwd_send.at[i], fwd_recv.at[i], sibling)
        forward.start()
        passes.append(forward)
    for forward in passes:
        forward.wait_recv()

    def score_pass(asked):
        query = asked[...].reshape(many, asked.shape[2])
        high = jnp.full((many, 128), -jnp.inf, jnp.float32)
        for j in range(positions // BLOCK):
            part = jnp.dot(
                query, root[:, j * BLOCK : (j + 1) * BLOCK], preferred_element_type=jnp.float32
            )
            scores[:, j * BLOCK : (j + 1) * BLOCK] = part
            for k in range(BLOCK // 128):
                high = jnp.maximum(high, part[:, k * 128 : (k + 1) * 128])
        wide = asked[...].astype(jnp.float32)
        place = me * tail + lax.broadcasted_iota(jnp.int32, (1, tail), 1)
        for r in range(reqs):
            mine = wide[:, r * heads : (r + 1) * heads, :]
            mine = mine.reshape(CHIPS * heads, asked.shape[2]).astype(jnp.bfloat16)
            part = jnp.dot(mine, suffix[picks[r]], preferred_element_type=jnp.float32)
            part = jnp.where(place < lengths[picks[r]], part, -jnp.inf)
            suffix_scores[:, r * heads : (r + 1) * heads, :] = part.reshape(CHIPS, heads, tail)
        whole = suffix_scores[...].reshape(many, tail)
        for k in range(tail // 128):
            high = jnp.maximum(high, whole[:, k * 128 : (k + 1) * 128])
        return jnp.max(high, axis=1, keepdims=True)

    def value_pass(top):
        lanes = jnp.zeros((many, 128), jnp.float32)
        out = jnp.zeros((many, LATENT), jnp.float32)
        for j in range(positions // BLOCK):
            weight = jnp.exp2((scores[:, j * BLOCK : (j + 1) * BLOCK] - top) * EXP2_SCALE)
            for k in range(BLOCK // 128):
                lanes = lanes + weight[:, k * 128 : (k + 1) * 128]
            out = out + lax.dot_general(
                weight.astype(jnp.bfloat16),
                root[:LATENT, j * BLOCK : (j + 1) * BLOCK],
                (((1,), (1,)), ((), ())),
                preferred_element_type=jnp.float32,
            )
        weight = jnp.exp2((suffix_scores[...].reshape(many, tail) - top) * EXP2_SCALE)
        for k in range(tail // 128):
            lanes = lanes + weight[:, k * 128 : (k + 1) * 128]
        weight = weight.reshape(CHIPS, rows, tail)
        pieces = []
        for r in range(reqs):
            mine = weight[:, r * heads : (r + 1) * heads, :]
            mine = mine.reshape(CHIPS * heads, tail).astype(jnp.bfloat16)
            part = lax.dot_general(
                mine,
                suffix[picks[r], :LATENT],
                (((1,), (1,)), ((), ())),
                preferred_element_type=jnp.float32,
            )
            pieces.append(part.reshape(CHIPS, 1, heads, LATENT))
        out = out + jnp.concatenate(pieces, axis=1).reshape(many, LATENT)
        return lanes, out

    top = score_pass(far)
    pair_top[...] = jnp.broadcast_to(top, (many, 128))
    lanes, out = value_pass(top)
    pair_sum[...] = lanes
    pair_out[...] = out.astype(jnp.bfloat16)
    pairs = [
        remote(pair_top, got_top, pair_send.at[0], pair_recv.at[0], sibling),
        remote(pair_sum, got_sum, pair_send.at[1], pair_recv.at[1], sibling),
        remote(pair_out, got_out, pair_send.at[2], pair_recv.at[2], sibling),
    ]
    for pair in pairs:
        pair.start()

    top = score_pass(near)
    for pair in pairs:
        pair.wait_recv()
    other_top = got_top[:, :1]
    joint = jnp.maximum(top, other_top)
    lanes, out = value_pass(joint)
    factor = jnp.exp2((other_top - joint) * EXP2_SCALE)
    lanes = lanes + got_sum[...] * factor
    out = out + got_out[...].astype(jnp.float32) * factor
    part_out[...] = out.astype(jnp.bfloat16).reshape(CHIPS, rows, LATENT)
    total = jnp.sum(lanes, axis=1, keepdims=True)
    row = lax.broadcasted_iota(jnp.int32, (rows, 128), 0)
    lane = lax.broadcasted_iota(jnp.int32, (rows, 128), 1)
    for j in range(CHIPS):
        here = slice(j * rows, (j + 1) * rows)
        stat = jnp.where(lane == row, joint[here], 0.0) + jnp.where(lane == row + rows, total[here], 0.0)
        part_stat[j] = jnp.sum(stat, axis=0, keepdims=True)

    sends = []
    for i, peer in enumerate(PEERS):
        device = target(peer)
        to = device // 2
        sends.append(
            remote(part_stat.at[to], all_stat.at[chip], stat_send.at[i], stat_recv.at[i], device)
        )
        sends.append(remote(part_out.at[to], all_out.at[chip], out_send.at[i], out_recv.at[i], device))
    for send in sends:
        send.start()
    all_out[chip] = part_out[chip]
    all_stat[chip] = part_stat[chip]
    for send in sends:
        send.wait_recv()

    stat = all_stat[...].reshape(CHIPS, 128)
    high = jnp.max(stat, axis=0, keepdims=True)
    share = jnp.exp2((stat - high) * EXP2_SCALE)
    sums = pltpu.roll(stat, 128 - rows, 1)
    share = share / jnp.sum(share * sums, axis=0, keepdims=True)
    result = jnp.zeros((rows, LATENT), jnp.float32)
    for j in range(CHIPS):
        column = jnp.sum(
            jnp.where(lane == row, share[j : j + 1], 0.0), axis=1, keepdims=True
        )
        result = result + all_out[j].astype(jnp.float32) * column
    o_ref[...] = result.astype(jnp.bfloat16)

    for copy in asks + passes + pairs + sends:
        copy.wait_send()


def local(queries, root_latent, suffix_latent, suffix_length, branch_pick):
    reqs, heads, width = queries.shape
    rows = reqs * heads
    positions = root_latent.shape[0]
    tail = suffix_latent.shape[1]
    many = CHIPS * rows
    count = len(PEERS)
    dma = pltpu.SemaphoreType.DMA
    out = pl.pallas_call(
        kernel,
        out_shape=jax.ShapeDtypeStruct((rows, LATENT), jnp.bfloat16),
        in_specs=[pl.BlockSpec(memory_space=pl.ANY)] * 3
        + [pl.BlockSpec(memory_space=pltpu.SMEM)] * 2,
        out_specs=pl.BlockSpec(memory_space=pltpu.VMEM),
        scratch_shapes=[
            pltpu.VMEM((width, positions), jnp.bfloat16),
            pltpu.VMEM((reqs, width, tail), jnp.bfloat16),
            pltpu.VMEM((CHIPS, rows, width), jnp.bfloat16),
            pltpu.VMEM((CHIPS, rows, width), jnp.bfloat16),
            pltpu.VMEM((many, positions), jnp.float32),
            pltpu.VMEM((CHIPS, rows, tail), jnp.float32),
            pltpu.VMEM((many, LATENT), jnp.bfloat16),
            pltpu.VMEM((many, 128), jnp.float32),
            pltpu.VMEM((many, 128), jnp.float32),
            pltpu.VMEM((many, LATENT), jnp.bfloat16),
            pltpu.VMEM((many, 128), jnp.float32),
            pltpu.VMEM((many, 128), jnp.float32),
            pltpu.VMEM((CHIPS, rows, LATENT), jnp.bfloat16),
            pltpu.VMEM((CHIPS, 1, 128), jnp.float32),
            pltpu.VMEM((CHIPS, rows, LATENT), jnp.bfloat16),
            pltpu.VMEM((CHIPS, 1, 128), jnp.float32),
            dma((2 + ROOT_PARTS,)),
            dma((count,)),
            dma((count,)),
            dma((count + 1,)),
            dma((count + 1,)),
            dma((3,)),
            dma((3,)),
            dma((count,)),
            dma((count,)),
            dma((count,)),
            dma((count,)),
        ],
        compiler_params=pltpu.CompilerParams(
            collective_id=0, has_side_effects=True, vmem_limit_bytes=56 * 2**20
        ),
    )(
        queries.reshape(rows, width),
        root_latent.T,
        suffix_latent.transpose(0, 2, 1),
        suffix_length,
        branch_pick,
    )
    return out.reshape(reqs, heads, LATENT)


def solution(mesh):
    return jax.shard_map(
        local,
        mesh=mesh,
        in_specs=(P("req", "pre", None), P("pre", None), P("req", "pre", None), P("req"), P("req")),
        out_specs=P("req", "pre", None),
        check_vma=False,
    )
```

```python
import functools

import jax
import jax.numpy as jnp
from jax import lax
from jax.experimental import pallas as pl
from jax.experimental.pallas import tpu as pltpu
from jax.sharding import PartitionSpec as P

MESH = pl.DeviceIdType.MESH
LATENT = 512
SCORE_SCALE = 192.0 ** (-0.5)
EXP2_SCALE = SCORE_SCALE * 1.4426950408889634
YS, XS = 4, 2
CHIPS = XS * YS
PEERS = {0: (1, 0), 1: (0, 1), 2: (0, 3), 4: (1, 1), 5: (1, 3), 6: (0, 2), 7: (1, 2)}
OWN = 3
NEXT, SECOND, THIRD = (0, 1, 2), (4, 5), (6, 7)
HALF = CHIPS // 2
BLOCK = 1024
FLOOR = -1e30
ROOT_PARTS = 4


def kernel(
    q_hbm,
    root_hbm,
    suffix_hbm,
    lengths,
    picks,
    o_ref,
    keys,
    values,
    suffix,
    branch_values,
    suffix_top,
    suffix_sum,
    suffix_out,
    near,
    far,
    pair_out,
    pair_top,
    pair_sum,
    got_out,
    got_top,
    got_sum,
    part_out,
    part_stat,
    all_out,
    all_stat,
    load_sem,
    ask_send,
    ask_recv,
    fwd_send,
    fwd_recv,
    pair_send,
    pair_recv,
    out_send,
    out_recv,
    stat_send,
    stat_recv,
):
    me = lax.axis_index("pre")
    core = me % 2
    chip = me // 2
    x, y = chip // YS, chip % YS
    sibling = me + 1 - 2 * core
    reqs = lengths.shape[0]
    rows, width = q_hbm.shape
    heads = rows // reqs
    half = HALF * rows
    positions = root_hbm.shape[1]
    tail = suffix_hbm.shape[2]

    def target(peer):
        dx, dy = peer
        return (((x + dx) % XS) * YS + (y + dy) % YS) * 2 + core

    def source(peer):
        dx, dy = peer
        return (((x + dx) % XS) * YS + (y + YS - dy) % YS) * 2 + core

    barrier = pltpu.get_barrier_semaphore()
    for peer in PEERS.values():
        pl.semaphore_signal(barrier, inc=1, device_id={"pre": target(peer)}, device_id_type=MESH)
    pl.semaphore_signal(barrier, inc=1, device_id={"pre": sibling}, device_id_type=MESH)

    own = pltpu.make_async_copy(q_hbm, near.at[OWN], load_sem.at[0])
    own.start()
    depth = width // ROOT_PARTS
    loads = [
        pltpu.make_async_copy(
            root_hbm.at[pl.ds(i * depth, depth)], keys.at[pl.ds(i * depth, depth)], load_sem.at[2 + i]
        )
        for i in range(ROOT_PARTS)
    ]
    loads.append(pltpu.make_async_copy(suffix_hbm, suffix, load_sem.at[1]))
    for load in loads:
        load.start()
    own.wait()
    pl.semaphore_wait(barrier, len(PEERS) + 1)

    def remote(src, dst, send, recv, device):
        return pltpu.make_async_remote_copy(
            src_ref=src,
            dst_ref=dst,
            send_sem=send,
            recv_sem=recv,
            device_id={"pre": device},
            device_id_type=MESH,
        )

    asks = {
        i: remote(near.at[OWN], near.at[i], ask_send.at[i], ask_recv.at[i], target(peer))
        for i, peer in PEERS.items()
    }
    passes = [
        remote(near.at[i], far.at[i], fwd_send.at[i], fwd_recv.at[i], sibling) for i in range(CHIPS)
    ]

    def pass_on(i):
        asks[i].wait_recv()
        passes[i].start()

    for ask in asks.values():
        ask.start()
    passes[OWN].start()
    for load in loads:
        load.wait()

    def turn(i, carry):
        at = pl.multiple_of(i * 512, 512)
        for k in range(4):
            values[pl.ds(at + k * 128, 128), :] = keys[:LATENT, pl.ds(at + k * 128, 128)].T
        return carry

    lax.fori_loop(0, positions // 512, turn, 0)
    for r in range(reqs):
        branch_values[r] = suffix[picks[r], :LATENT].T

    place = me * tail + lax.broadcasted_iota(jnp.int32, (1, tail), 1)

    calls = []

    def lane_sums(weight):
        return sum(weight[:, k * 128 : (k + 1) * 128] for k in range(weight.shape[1] // 128))

    def joined(first, second):
        top = jnp.maximum(first[0], second[0])
        scales = [jnp.exp2((state[0] - top) * EXP2_SCALE) for state in (first, second)]
        return top, *(
            first[i].astype(jnp.float32) * scales[0] + second[i].astype(jnp.float32) * scales[1]
            for i in (1, 2)
        )

    def attend_suffix(r):
        asked = [ref[:, r * heads : (r + 1) * heads].astype(jnp.float32) for ref in (far, near)]
        asked = jnp.concatenate(asked).reshape(2 * CHIPS * heads, width).astype(jnp.bfloat16)
        part = jnp.dot(asked, suffix[picks[r]], preferred_element_type=jnp.float32)
        part = jnp.where(place < lengths[picks[r]], part, -jnp.inf)
        top = jnp.maximum(jnp.max(part, axis=1, keepdims=True), FLOOR)
        weight = jnp.exp2((part - top) * EXP2_SCALE)
        out = jnp.dot(
            weight.astype(jnp.bfloat16), branch_values[r], preferred_element_type=jnp.float32
        )
        for ref, got in (
            (suffix_top, jnp.broadcast_to(top, (top.shape[0], 128))),
            (suffix_sum, lane_sums(weight)),
            (suffix_out, out),
        ):
            ref[:, r * heads : (r + 1) * heads] = got.reshape(2 * CHIPS, heads, got.shape[1])

    def suffix_state(k):
        here = slice(k * HALF, (k + 1) * HALF)
        top, sums, out = (
            ref[here].reshape(half, ref.shape[2]) for ref in (suffix_top, suffix_sum, suffix_out)
        )
        return top[:, :1], sums, out

    def attend(asked, state, between):
        query = asked.reshape(asked.shape[0] * rows, width)

        def score(j):
            return jnp.dot(
                query, keys[:, j * BLOCK : (j + 1) * BLOCK], preferred_element_type=jnp.float32
            )

        count = positions // BLOCK
        part = score(0)
        for j in range(count):
            following = score(j + 1) if j + 1 < count else None
            high = jnp.max(part, axis=1, keepdims=True)
            if state is not None:
                high = jnp.maximum(state[0], high)
                factor = jnp.exp2((state[0] - high) * EXP2_SCALE)
            weight = jnp.exp2((part - high) * EXP2_SCALE)
            sums = lane_sums(weight)
            out = jnp.dot(
                weight.astype(jnp.bfloat16),
                values[j * BLOCK : (j + 1) * BLOCK, :],
                preferred_element_type=jnp.float32,
            )
            if state is not None:
                sums = sums + state[1] * factor
                out = out + state[2] * factor
            state, part = (high, sums, out), following
            for step in between.get(j, ()):
                step()
        return state

    pairs = {}

    def to_sibling(k, state):
        top, sums, out = state
        here = pl.ds(k * half, half)
        pair_top[here] = jnp.broadcast_to(top, (half, 128))
        pair_sum[here] = sums
        pair_out[here] = out.astype(jnp.bfloat16)
        pairs[k] = [
            remote(src.at[here], dst.at[here], pair_send.at[3 * k + i], pair_recv.at[3 * k + i], sibling)
            for i, (src, dst) in enumerate(
                ((pair_top, got_top), (pair_sum, got_sum), (pair_out, got_out))
            )
        ]
        for copy in pairs[k]:
            copy.start()

    row = lax.broadcasted_iota(jnp.int32, (rows, 128), 0)
    lane = lax.broadcasted_iota(jnp.int32, (rows, 128), 1)
    sends = []

    def to_owners(k, state):
        here = pl.ds(k * half, half)
        for copy in pairs[k]:
            copy.wait_recv()
        joint, sums, out = joined(state, (got_top[here][:, :1], got_sum[here], got_out[here]))
        out = out.astype(jnp.bfloat16)
        total = jnp.sum(sums, axis=1, keepdims=True)
        for j in reversed(range(HALF)):
            slot = k * HALF + j
            part = slice(j * rows, (j + 1) * rows)
            stat = jnp.where(lane == row, joint[part], 0.0)
            stat = stat + jnp.where(lane == row + rows, total[part], 0.0)
            stat = jnp.sum(stat, axis=0, keepdims=True)
            if slot == OWN:
                all_out[slot] = out[part]
                all_stat[slot] = stat
                continue
            part_out[slot] = out[part]
            part_stat[slot] = stat
            device = source(PEERS[slot])
            pair = [
                remote(
                    part_out.at[slot], all_out.at[slot], out_send.at[slot], out_recv.at[slot], device
                ),
                remote(
                    part_stat.at[slot], all_stat.at[slot], stat_send.at[slot], stat_recv.at[slot], device
                ),
            ]
            for copy in pair:
                copy.start()
            sends.extend(pair)

    def hook(*slots):
        return [functools.partial(pass_on, i) for i in slots]

    for i in NEXT:
        pass_on(i)
    own_first = attend(near[:HALF], None, {1: hook(*SECOND)})
    for i in (*NEXT, OWN):
        passes[i].wait_recv()
    first = attend(far[:HALF], None, {0: hook(*THIRD)})
    for i in (*SECOND, *THIRD):
        passes[i].wait_recv()
    suffixes = {j: [functools.partial(attend_suffix, j)] for j in range(reqs)}
    second = attend(far[HALF:], None, suffixes)
    to_sibling(1, joined(second, suffix_state(1)))
    to_sibling(0, joined(first, suffix_state(0)))
    own_second = attend(near[HALF:], suffix_state(3), {})
    to_owners(1, own_second)
    to_owners(0, joined(own_first, suffix_state(2)))
    for send in sends:
        send.wait_recv()

    stat = all_stat[...].reshape(CHIPS, 128)
    high = jnp.max(stat, axis=0, keepdims=True)
    share = jnp.exp2((stat - high) * EXP2_SCALE)
    totals = pltpu.roll(stat, 128 - rows, 1)
    share = share / jnp.sum(share * totals, axis=0, keepdims=True)
    result = jnp.zeros((rows, LATENT), jnp.float32)
    for j in range(CHIPS):
        column = jnp.sum(jnp.where(lane == row, share[j : j + 1], 0.0), axis=1, keepdims=True)
        result = result + all_out[j].astype(jnp.float32) * column
    o_ref[...] = result.astype(jnp.bfloat16)

    for copy in [*asks.values(), *passes, *pairs[0], *pairs[1], *sends]:
        copy.wait_send()


def local(queries, root_latent, suffix_latent, suffix_length, branch_pick):
    reqs, heads, width = queries.shape
    rows = reqs * heads
    many = CHIPS * rows
    positions = root_latent.shape[0]
    tail = suffix_latent.shape[1]
    dma = pltpu.SemaphoreType.DMA
    out = pl.pallas_call(
        kernel,
        out_shape=jax.ShapeDtypeStruct((rows, LATENT), jnp.bfloat16),
        in_specs=[pl.BlockSpec(memory_space=pl.ANY)] * 3
        + [pl.BlockSpec(memory_space=pltpu.SMEM)] * 2,
        out_specs=pl.BlockSpec(memory_space=pltpu.VMEM),
        scratch_shapes=[
            pltpu.VMEM((width, positions), jnp.bfloat16),
            pltpu.VMEM((positions, LATENT), jnp.bfloat16),
            pltpu.VMEM((reqs, width, tail), jnp.bfloat16),
            pltpu.VMEM((reqs, tail, LATENT), jnp.bfloat16),
            pltpu.VMEM((2 * CHIPS, rows, 128), jnp.float32),
            pltpu.VMEM((2 * CHIPS, rows, 128), jnp.float32),
            pltpu.VMEM((2 * CHIPS, rows, LATENT), jnp.float32),
            pltpu.VMEM((CHIPS, rows, width), jnp.bfloat16),
            pltpu.VMEM((CHIPS, rows, width), jnp.bfloat16),
            pltpu.VMEM((many, LATENT), jnp.bfloat16),
            pltpu.VMEM((many, 128), jnp.float32),
            pltpu.VMEM((many, 128), jnp.float32),
            pltpu.VMEM((many, LATENT), jnp.bfloat16),
            pltpu.VMEM((many, 128), jnp.float32),
            pltpu.VMEM((many, 128), jnp.float32),
            pltpu.VMEM((CHIPS, rows, LATENT), jnp.bfloat16),
            pltpu.VMEM((CHIPS, 1, 128), jnp.float32),
            pltpu.VMEM((CHIPS, rows, LATENT), jnp.bfloat16),
            pltpu.VMEM((CHIPS, 1, 128), jnp.float32),
            dma((2 + ROOT_PARTS,)),
            dma((CHIPS,)),
            dma((CHIPS,)),
            dma((CHIPS,)),
            dma((CHIPS,)),
            dma((6,)),
            dma((6,)),
            dma((CHIPS,)),
            dma((CHIPS,)),
            dma((CHIPS,)),
            dma((CHIPS,)),
        ],
        compiler_params=pltpu.CompilerParams(
            collective_id=0, has_side_effects=True, vmem_limit_bytes=56 * 2**20
        ),
    )(
        queries.reshape(rows, width),
        root_latent.T,
        suffix_latent.transpose(0, 2, 1),
        suffix_length,
        branch_pick,
    )
    return out.reshape(reqs, heads, LATENT)


def solution(mesh):
    return jax.shard_map(
        local,
        mesh=mesh,
        in_specs=(P("req", "pre", None), P("pre", None), P("req", "pre", None), P("req"), P("req")),
        out_specs=P("req", "pre", None),
        check_vma=False,
    )
```

```python
import functools

import jax
import jax.numpy as jnp
from jax import lax
from jax.experimental import pallas as pl
from jax.experimental.pallas import tpu as pltpu
from jax.sharding import PartitionSpec as P

MESH = pl.DeviceIdType.MESH
LATENT = 512
SCORE_SCALE = 192.0 ** (-0.5)
EXP2_SCALE = SCORE_SCALE * 1.4426950408889634
YS, XS = 4, 2
CHIPS = XS * YS
PEERS = {0: (1, 0), 1: (0, 1), 2: (0, 3), 4: (1, 1), 5: (1, 3), 6: (0, 2), 7: (1, 2)}
OWN = 3
NEXT, SECOND, THIRD = (0, 1, 2), (4, 5), (6, 7)
HALF = CHIPS // 2
BLOCK = 1024
SUFFIX_AT = 3
ROOT_PARTS = 4


def kernel(
    q_hbm,
    root_hbm,
    suffix_hbm,
    lengths,
    picks,
    all_out,
    all_stat,
    keys,
    values,
    suffix,
    branch_values,
    near,
    far,
    part_out,
    part_stat,
    load_sem,
    ask_send,
    ask_recv,
    fwd_send,
    fwd_recv,
    out_send,
    out_recv,
    stat_send,
    stat_recv,
):
    me = lax.axis_index("pre")
    core = me % 2
    chip = me // 2
    x, y = chip // YS, chip % YS

    def other_core(device):
        return device + 1 - 2 * core

    sibling = other_core(me)
    reqs = lengths.shape[0]
    rows, width = q_hbm.shape
    heads = rows // reqs
    half = HALF * rows
    positions = root_hbm.shape[1]
    tail = suffix_hbm.shape[2]

    def target(peer):
        dx, dy = peer
        return (((x + dx) % XS) * YS + (y + dy) % YS) * 2 + core

    def source(peer):
        dx, dy = peer
        return (((x + dx) % XS) * YS + (y + YS - dy) % YS) * 2 + core

    barrier = pltpu.get_barrier_semaphore()
    partners = [*(target(peer) for peer in reversed(PEERS.values())), sibling]
    for partner in partners:
        pl.semaphore_signal(barrier, inc=1, device_id={"pre": partner}, device_id_type=MESH)

    own = pltpu.make_async_copy(q_hbm, near.at[OWN], load_sem.at[0])
    own.start()
    depth = width // ROOT_PARTS
    loads = [
        pltpu.make_async_copy(
            root_hbm.at[pl.ds(i * depth, depth)], keys.at[pl.ds(i * depth, depth)], load_sem.at[2 + i]
        )
        for i in range(ROOT_PARTS)
    ]
    loads.append(pltpu.make_async_copy(suffix_hbm, suffix, load_sem.at[1]))
    for load in loads:
        load.start()
    own.wait()
    pl.semaphore_wait(barrier, len(partners))

    def remote(src, dst, send, recv, device):
        return pltpu.make_async_remote_copy(
            src_ref=src,
            dst_ref=dst,
            send_sem=send,
            recv_sem=recv,
            device_id={"pre": device},
            device_id_type=MESH,
        )

    asks = {
        i: remote(near.at[OWN], near.at[i], ask_send.at[i], ask_recv.at[i], target(peer))
        for i, peer in PEERS.items()
    }
    passes = [
        remote(near.at[i], far.at[i], fwd_send.at[i], fwd_recv.at[i], sibling) for i in range(CHIPS)
    ]

    def pass_on(i):
        asks[i].wait_recv()
        passes[i].start()

    for ask in asks.values():
        ask.start()
    passes[OWN].start()
    for load in loads:
        load.wait()

    def turn(i, carry):
        at = pl.multiple_of(i * 512, 512)
        for k in range(4):
            values[pl.ds(at + k * 128, 128), :] = keys[:LATENT, pl.ds(at + k * 128, 128)].T
        return carry

    lax.fori_loop(0, positions // 512, turn, 0)
    for r in range(reqs):
        branch_values[r] = suffix[picks[r], :LATENT].T

    place = me * tail + lax.broadcasted_iota(jnp.int32, (1, tail), 1)

    calls = []

    def lane_sums(weight):
        return sum(weight[:, k * 128 : (k + 1) * 128] for k in range(weight.shape[1] // 128))

    def by_request(part):
        part = part.astype(jnp.float32).reshape(HALF, rows, part.shape[-1])
        return [
            part[:, r * heads : (r + 1) * heads].reshape(HALF * heads, part.shape[-1])
            for r in range(reqs)
        ]

    def by_row(parts):
        parts = [part.reshape(HALF, 1, heads, part.shape[-1]) for part in parts]
        return jnp.concatenate(parts, axis=1).reshape(half, parts[0].shape[-1])

    def attend(asked, between):
        query = asked.reshape(half, width)

        def root_score(j):
            return jnp.dot(
                query, keys[:, j * BLOCK : (j + 1) * BLOCK], preferred_element_type=jnp.float32
            )

        def root_product(j, weight):
            return jnp.dot(
                weight.astype(jnp.bfloat16),
                values[j * BLOCK : (j + 1) * BLOCK, :],
                preferred_element_type=jnp.float32,
            )

        def suffix_score():
            parts = []
            for r, mine in enumerate(by_request(asked)):
                part = jnp.dot(
                    mine.astype(jnp.bfloat16), suffix[picks[r]], preferred_element_type=jnp.float32
                )
                parts.append(jnp.where(place < lengths[picks[r]], part, -jnp.inf))
            return by_row(parts)

        def suffix_product(weight):
            return by_row(
                [
                    jnp.dot(
                        mine.astype(jnp.bfloat16), branch_values[r], preferred_element_type=jnp.float32
                    )
                    for r, mine in enumerate(by_request(weight))
                ]
            )

        steps = [
            (functools.partial(root_score, j), functools.partial(root_product, j))
            for j in range(positions // BLOCK)
        ]
        steps.insert(SUFFIX_AT, (suffix_score, suffix_product))
        part = steps[0][0]()
        state = None
        for j, (_, product) in enumerate(steps):
            following = steps[j + 1][0]() if j + 1 < len(steps) else None
            high = jnp.max(part, axis=1, keepdims=True)
            if state is not None:
                high = jnp.maximum(state[0], high)
                factor = jnp.exp2((state[0] - high) * EXP2_SCALE)
            weight = jnp.exp2((part - high) * EXP2_SCALE)
            sums, out = lane_sums(weight), product(weight)
            if state is not None:
                sums = sums + state[1] * factor
                out = out + state[2] * factor
            state, part = (high, sums, out), following
            for step in between.get(j, ()):
                step()
        return state

    row = lax.broadcasted_iota(jnp.int32, (rows, 128), 0)
    lane = lax.broadcasted_iota(jnp.int32, (rows, 128), 1)
    sends, kept = [], []

    def to_owners(near_rows, k, state):
        joint, sums, out = state
        out = out.astype(jnp.bfloat16)
        total = jnp.sum(sums, axis=1, keepdims=True)
        for j in reversed(range(HALF)):
            slot = k * HALF + j
            at = slot if near_rows else CHIPS + slot
            part = slice(j * rows, (j + 1) * rows)
            stat = jnp.where(lane == row, joint[part], 0.0)
            stat = stat + jnp.where(lane == row + rows, total[part], 0.0)
            stat = jnp.sum(stat, axis=0, keepdims=True)
            part_out[at] = out[part]
            part_stat[at] = stat
            if near_rows and slot == OWN:
                pair = [
                    pltpu.make_async_copy(part_out.at[at], all_out.at[at], load_sem.at[0]),
                    pltpu.make_async_copy(part_stat.at[at], all_stat.at[at], load_sem.at[1]),
                ]
                for copy in pair:
                    copy.start()
                kept.extend(pair)
                continue
            device = me if slot == OWN else source(PEERS[slot])
            device = device if near_rows else other_core(device)
            pair = [
                remote(part_out.at[at], all_out.at[at], out_send.at[at], out_recv.at[at], device),
                remote(part_stat.at[at], all_stat.at[at], stat_send.at[at], stat_recv.at[at], device),
            ]
            for copy in pair:
                copy.start()
            sends.extend(pair)

    def hook(*slots):
        return [functools.partial(pass_on, i) for i in slots]

    for i in NEXT:
        pass_on(i)
    state = attend(near[:HALF], {1: hook(*SECOND)})
    for i in THIRD:
        pass_on(i)
    to_owners(True, 0, state)
    state = attend(near[HALF:], {})
    for i in range(CHIPS):
        passes[i].wait_recv()
    to_owners(True, 1, state)
    state = attend(far[HALF:], {})
    to_owners(False, 1, state)
    state = attend(far[:HALF], {})
    to_owners(False, 0, state)
    for send in sends:
        send.wait_recv()
    for copy in kept:
        copy.wait()

    for copy in [*asks.values(), *passes, *sends]:
        copy.wait_send()


def combine(all_out, all_stat, o_ref):
    rows = o_ref.shape[0]
    row = lax.broadcasted_iota(jnp.int32, (rows, 128), 0)
    lane = lax.broadcasted_iota(jnp.int32, (rows, 128), 1)
    stat = all_stat[...].reshape(2 * CHIPS, 128)
    high = jnp.max(stat, axis=0, keepdims=True)
    share = jnp.exp2((stat - high) * EXP2_SCALE)
    totals = pltpu.roll(stat, 128 - rows, 1)
    share = share / jnp.sum(share * totals, axis=0, keepdims=True)
    result = jnp.zeros((rows, LATENT), jnp.float32)
    for j in range(2 * CHIPS):
        column = jnp.sum(jnp.where(lane == row, share[j : j + 1], 0.0), axis=1, keepdims=True)
        result = result + all_out[j].astype(jnp.float32) * column
    o_ref[...] = result.astype(jnp.bfloat16)


def local(queries, root_latent, suffix_latent, suffix_length, branch_pick):
    reqs, heads, width = queries.shape
    rows = reqs * heads
    positions = root_latent.shape[0]
    tail = suffix_latent.shape[1]
    dma = pltpu.SemaphoreType.DMA
    parts = pl.pallas_call(
        kernel,
        out_shape=[
            jax.ShapeDtypeStruct((2 * CHIPS, rows, LATENT), jnp.bfloat16),
            jax.ShapeDtypeStruct((2 * CHIPS, 1, 128), jnp.float32),
        ],
        in_specs=[pl.BlockSpec(memory_space=pl.ANY)] * 3
        + [pl.BlockSpec(memory_space=pltpu.SMEM)] * 2,
        out_specs=[pl.BlockSpec(memory_space=pl.ANY)] * 2,
        scratch_shapes=[
            pltpu.VMEM((width, positions), jnp.bfloat16),
            pltpu.VMEM((positions, LATENT), jnp.bfloat16),
            pltpu.VMEM((reqs, width, tail), jnp.bfloat16),
            pltpu.VMEM((reqs, tail, LATENT), jnp.bfloat16),
            pltpu.VMEM((CHIPS, rows, width), jnp.bfloat16),
            pltpu.VMEM((CHIPS, rows, width), jnp.bfloat16),
            pltpu.VMEM((2 * CHIPS, rows, LATENT), jnp.bfloat16),
            pltpu.VMEM((2 * CHIPS, 1, 128), jnp.float32),
            dma((2 + ROOT_PARTS,)),
            dma((CHIPS,)),
            dma((CHIPS,)),
            dma((CHIPS,)),
            dma((CHIPS,)),
            dma((2 * CHIPS,)),
            dma((2 * CHIPS,)),
            dma((2 * CHIPS,)),
            dma((2 * CHIPS,)),
        ],
        compiler_params=pltpu.CompilerParams(
            collective_id=0, has_side_effects=True, vmem_limit_bytes=56 * 2**20
        ),
    )(
        queries.reshape(rows, width),
        root_latent.T,
        suffix_latent.transpose(0, 2, 1),
        suffix_length,
        branch_pick,
    )
    out = pl.pallas_call(
        combine,
        out_shape=jax.ShapeDtypeStruct((rows, LATENT), jnp.bfloat16),
        in_specs=[pl.BlockSpec(memory_space=pltpu.VMEM)] * 2,
        out_specs=pl.BlockSpec(memory_space=pltpu.VMEM),
    )(*parts)
    return out.reshape(reqs, heads, LATENT)


def solution(mesh):
    return jax.shard_map(
        local,
        mesh=mesh,
        in_specs=(P("req", "pre", None), P("pre", None), P("req", "pre", None), P("req"), P("req")),
        out_specs=P("req", "pre", None),
        check_vma=False,
    )
```

```python
import functools

import jax
import jax.numpy as jnp
from jax import lax
from jax.experimental import pallas as pl
from jax.experimental.pallas import tpu as pltpu
from jax.sharding import PartitionSpec as P

MESH = pl.DeviceIdType.MESH
LATENT = 512
SCORE_SCALE = 192.0 ** (-0.5)
EXP2_SCALE = SCORE_SCALE * 1.4426950408889634
YS, XS = 4, 2
CHIPS = XS * YS
PEERS = {0: (1, 0), 1: (0, 1), 2: (0, 3), 4: (1, 1), 5: (1, 3), 6: (0, 2), 7: (1, 2)}
OWN = 3
NEXT, SECOND, THIRD = (0, 1, 2), (4, 5), (6, 7)
HALF = CHIPS // 2
BLOCK = 1024
SUFFIX_AT = 3
ROOT_PARTS = 4


def kernel(
    q_hbm,
    root_hbm,
    suffix_hbm,
    lengths,
    picks,
    all_out,
    all_stat,
    keys,
    values,
    suffix,
    branch_values,
    near,
    far,
    part_out,
    part_stat,
    load_sem,
    ask_send,
    ask_recv,
    fwd_send,
    fwd_recv,
    out_send,
    out_recv,
    stat_send,
    stat_recv,
):
    me = lax.axis_index("pre")
    core = me % 2
    chip = me // 2
    x, y = chip // YS, chip % YS

    def other_core(device):
        return device + 1 - 2 * core

    sibling = other_core(me)
    reqs = lengths.shape[0]
    rows, width = q_hbm.shape
    heads = rows // reqs
    half = HALF * rows
    positions = root_hbm.shape[1]
    tail = suffix_hbm.shape[2]

    def target(peer):
        dx, dy = peer
        return (((x + dx) % XS) * YS + (y + dy) % YS) * 2 + core

    def source(peer):
        dx, dy = peer
        return (((x + dx) % XS) * YS + (y + YS - dy) % YS) * 2 + core

    barrier = pltpu.get_barrier_semaphore()
    partners = [*(target(peer) for peer in reversed(PEERS.values())), sibling]
    for partner in partners:
        pl.semaphore_signal(barrier, inc=1, device_id={"pre": partner}, device_id_type=MESH)

    own = pltpu.make_async_copy(q_hbm, near.at[OWN], load_sem.at[0])
    own.start()
    depth = width // ROOT_PARTS
    loads = [
        pltpu.make_async_copy(
            root_hbm.at[pl.ds(i * depth, depth)], keys.at[pl.ds(i * depth, depth)], load_sem.at[2 + i]
        )
        for i in range(ROOT_PARTS)
    ]
    loads.append(pltpu.make_async_copy(suffix_hbm, suffix, load_sem.at[1]))
    for load in loads:
        load.start()
    own.wait()
    pl.semaphore_wait(barrier, len(partners))

    def remote(src, dst, send, recv, device):
        return pltpu.make_async_remote_copy(
            src_ref=src,
            dst_ref=dst,
            send_sem=send,
            recv_sem=recv,
            device_id={"pre": device},
            device_id_type=MESH,
        )

    asks = {
        i: remote(near.at[OWN], near.at[i], ask_send, ask_recv.at[i], target(peer))
        for i, peer in PEERS.items()
    }
    passes = [
        remote(near.at[i], far.at[i], fwd_send, fwd_recv, sibling) for i in range(CHIPS)
    ]

    def pass_on(i):
        asks[i].wait_recv()
        passes[i].start()

    for ask in asks.values():
        ask.start()
    passes[OWN].start()
    for load in loads:
        load.wait()

    def turn(i, carry):
        at = pl.multiple_of(i * 512, 512)
        for k in range(4):
            values[pl.ds(at + k * 128, 128), :] = keys[:LATENT, pl.ds(at + k * 128, 128)].T
        return carry

    lax.fori_loop(0, positions // 512, turn, 0)
    for r in range(reqs):
        branch_values[r] = suffix[picks[r], :LATENT].T

    place = me * tail + lax.broadcasted_iota(jnp.int32, (1, tail), 1)

    calls = []

    def lane_sums(weight):
        return sum(weight[:, k * 128 : (k + 1) * 128] for k in range(weight.shape[1] // 128))

    def by_request(part):
        part = part.astype(jnp.float32).reshape(HALF, rows, part.shape[-1])
        return [
            part[:, r * heads : (r + 1) * heads].reshape(HALF * heads, part.shape[-1])
            for r in range(reqs)
        ]

    def by_row(parts):
        parts = [part.reshape(HALF, 1, heads, part.shape[-1]) for part in parts]
        return jnp.concatenate(parts, axis=1).reshape(half, parts[0].shape[-1])

    def attend(asked, between):
        query = asked.reshape(half, width)

        def root_score(j):
            return jnp.dot(
                query, keys[:, j * BLOCK : (j + 1) * BLOCK], preferred_element_type=jnp.float32
            )

        def root_product(j, weight):
            return jnp.dot(
                weight.astype(jnp.bfloat16),
                values[j * BLOCK : (j + 1) * BLOCK, :],
                preferred_element_type=jnp.float32,
            )

        def suffix_score():
            parts = []
            for r, mine in enumerate(by_request(asked)):
                part = jnp.dot(
                    mine.astype(jnp.bfloat16), suffix[picks[r]], preferred_element_type=jnp.float32
                )
                parts.append(jnp.where(place < lengths[picks[r]], part, -jnp.inf))
            return by_row(parts)

        def suffix_product(weight):
            return by_row(
                [
                    jnp.dot(
                        mine.astype(jnp.bfloat16), branch_values[r], preferred_element_type=jnp.float32
                    )
                    for r, mine in enumerate(by_request(weight))
                ]
            )

        steps = [
            (functools.partial(root_score, j), functools.partial(root_product, j))
            for j in range(positions // BLOCK)
        ]
        steps.insert(SUFFIX_AT, (suffix_score, suffix_product))
        part = steps[0][0]()
        state = None
        for j, (_, product) in enumerate(steps):
            following = steps[j + 1][0]() if j + 1 < len(steps) else None
            high = jnp.max(part, axis=1, keepdims=True)
            if state is not None:
                high = jnp.maximum(state[0], high)
                factor = jnp.exp2((state[0] - high) * EXP2_SCALE)
            weight = jnp.exp2((part - high) * EXP2_SCALE)
            sums, out = lane_sums(weight), product(weight)
            if state is not None:
                sums = sums + state[1] * factor
                out = out + state[2] * factor
            state, part = (high, sums, out), following
            for step in between.get(j, ()):
                step()
        return state

    row = lax.broadcasted_iota(jnp.int32, (rows, 128), 0)
    lane = lax.broadcasted_iota(jnp.int32, (rows, 128), 1)
    kept = []

    def store(near_rows, k, state):
        joint, sums, out = state
        base = (0 if near_rows else CHIPS) + k * HALF
        part_out[base : base + HALF] = out.astype(jnp.bfloat16).reshape(HALF, rows, LATENT)
        total = jnp.sum(sums, axis=1, keepdims=True)
        for j in range(HALF):
            part = slice(j * rows, (j + 1) * rows)
            stat = jnp.where(lane == row, joint[part], 0.0)
            stat = stat + jnp.where(lane == row + rows, total[part], 0.0)
            part_stat[base + j] = jnp.sum(stat, axis=0, keepdims=True)

    def send(near_rows, k):
        for slot in reversed(range(k * HALF, (k + 1) * HALF)):
            at = slot if near_rows else CHIPS + slot
            if near_rows and slot == OWN:
                pair = [
                    pltpu.make_async_copy(part_out.at[at], all_out.at[at], load_sem.at[0]),
                    pltpu.make_async_copy(part_stat.at[at], all_stat.at[at], load_sem.at[1]),
                ]
                kept.extend(pair)
            else:
                device = me if slot == OWN else source(PEERS[slot])
                device = device if near_rows else other_core(device)
                pair = [
                    remote(part_out.at[at], all_out.at[at], out_send, out_recv, device),
                    remote(part_stat.at[at], all_stat.at[at], stat_send, stat_recv, device),
                ]
            for copy in pair:
                copy.start()

    def hook(*slots):
        return [functools.partial(pass_on, i) for i in slots]

    for i in NEXT:
        pass_on(i)
    state = attend(near[:HALF], {1: hook(*SECOND)})
    for i in THIRD:
        pass_on(i)
    store(True, 0, state)
    send(True, 0)
    state = attend(near[HALF:], {})
    every_pass = remote(near, far, fwd_send, fwd_recv, sibling)
    every_pass.wait_recv()
    store(True, 1, state)
    send(True, 1)
    state = attend(far[HALF:], {})
    store(False, 1, state)
    send(False, 1)
    state = attend(far[:HALF], {})
    store(False, 0, state)
    send(False, 0)
    most = pl.ds(0, 2 * CHIPS - 1)
    outs = remote(part_out.at[most], all_out.at[most], out_send, out_recv, sibling)
    stats = remote(part_stat.at[most], all_stat.at[most], stat_send, stat_recv, sibling)
    others = pl.ds(0, len(PEERS))
    every_ask = remote(near.at[others], near.at[others], ask_send, ask_recv.at[OWN], sibling)
    for copy in (every_ask, every_pass, outs, stats):
        copy.wait_send()
    for copy in kept:
        copy.wait()
    outs.wait_recv()
    stats.wait_recv()


def combine(all_out, all_stat, o_ref):
    rows = o_ref.shape[0]
    row = lax.broadcasted_iota(jnp.int32, (rows, 128), 0)
    lane = lax.broadcasted_iota(jnp.int32, (rows, 128), 1)
    stat = all_stat[...].reshape(2 * CHIPS, 128)
    high = jnp.max(stat, axis=0, keepdims=True)
    share = jnp.exp2((stat - high) * EXP2_SCALE)
    totals = pltpu.roll(stat, 128 - rows, 1)
    share = share / jnp.sum(share * totals, axis=0, keepdims=True)
    result = jnp.zeros((rows, LATENT), jnp.float32)
    for j in range(2 * CHIPS):
        column = jnp.sum(jnp.where(lane == row, share[j : j + 1], 0.0), axis=1, keepdims=True)
        result = result + all_out[j].astype(jnp.float32) * column
    o_ref[...] = result.astype(jnp.bfloat16)


def local(queries, root_latent, suffix_latent, suffix_length, branch_pick):
    reqs, heads, width = queries.shape
    rows = reqs * heads
    positions = root_latent.shape[0]
    tail = suffix_latent.shape[1]
    dma = pltpu.SemaphoreType.DMA
    parts = pl.pallas_call(
        kernel,
        out_shape=[
            jax.ShapeDtypeStruct((2 * CHIPS, rows, LATENT), jnp.bfloat16),
            jax.ShapeDtypeStruct((2 * CHIPS, 1, 128), jnp.float32),
        ],
        in_specs=[pl.BlockSpec(memory_space=pl.ANY)] * 3
        + [pl.BlockSpec(memory_space=pltpu.SMEM)] * 2,
        out_specs=[pl.BlockSpec(memory_space=pl.ANY)] * 2,
        scratch_shapes=[
            pltpu.VMEM((width, positions), jnp.bfloat16),
            pltpu.VMEM((positions, LATENT), jnp.bfloat16),
            pltpu.VMEM((reqs, width, tail), jnp.bfloat16),
            pltpu.VMEM((reqs, tail, LATENT), jnp.bfloat16),
            pltpu.VMEM((CHIPS, rows, width), jnp.bfloat16),
            pltpu.VMEM((CHIPS, rows, width), jnp.bfloat16),
            pltpu.VMEM((2 * CHIPS, rows, LATENT), jnp.bfloat16),
            pltpu.VMEM((2 * CHIPS, 1, 128), jnp.float32),
            dma((2 + ROOT_PARTS,)),
            dma,
            dma((CHIPS,)),
            dma,
            dma,
            dma,
            dma,
            dma,
            dma,
        ],
        compiler_params=pltpu.CompilerParams(
            collective_id=0, has_side_effects=True, vmem_limit_bytes=56 * 2**20
        ),
    )(
        queries.reshape(rows, width),
        root_latent.T,
        suffix_latent.transpose(0, 2, 1),
        suffix_length,
        branch_pick,
    )
    out = pl.pallas_call(
        combine,
        out_shape=jax.ShapeDtypeStruct((rows, LATENT), jnp.bfloat16),
        in_specs=[pl.BlockSpec(memory_space=pltpu.VMEM)] * 2,
        out_specs=pl.BlockSpec(memory_space=pltpu.VMEM),
    )(*parts)
    return out.reshape(reqs, heads, LATENT)


def solution(mesh):
    return jax.shard_map(
        local,
        mesh=mesh,
        in_specs=(P("req", "pre", None), P("pre", None), P("req", "pre", None), P("req"), P("req")),
        out_specs=P("req", "pre", None),
        check_vma=False,
    )
```

```python
import functools

import jax
import jax.numpy as jnp
from jax import lax
from jax.experimental import pallas as pl
from jax.experimental.pallas import tpu as pltpu
from jax.sharding import PartitionSpec as P

MESH = pl.DeviceIdType.MESH
LATENT = 512
SCORE_SCALE = 192.0 ** (-0.5)
EXP2_SCALE = SCORE_SCALE * 1.4426950408889634
YS, XS = 4, 2
CHIPS = XS * YS
PEERS = {0: (1, 0), 1: (0, 1), 2: (0, 3), 4: (1, 1), 5: (1, 3), 6: (0, 2), 7: (1, 2)}
OWN = 3
NEXT, SECOND, THIRD = (0, 1, 2), (4, 5), (6, 7)
HALF = CHIPS // 2
BLOCK = 2048
SUFFIX_AT = 1
FLOOR = -1e30
ROOT_PARTS = 4


def kernel(
    q_hbm,
    root_hbm,
    suffix_hbm,
    lengths,
    picks,
    all_out,
    all_stat,
    keys,
    values,
    suffix,
    branch_values,
    near,
    far,
    part_out,
    part_stat,
    load_sem,
    ask_send,
    ask_recv,
    fwd_send,
    fwd_recv,
    out_send,
    out_recv,
    stat_send,
    stat_recv,
):
    me = lax.axis_index("pre")
    core = me % 2
    chip = me // 2
    x, y = chip // YS, chip % YS

    def other_core(device):
        return device + 1 - 2 * core

    sibling = other_core(me)
    reqs = lengths.shape[0]
    rows, width = q_hbm.shape
    heads = rows // reqs
    half = HALF * rows
    positions = root_hbm.shape[1]
    tail = suffix_hbm.shape[2]

    def target(peer):
        dx, dy = peer
        return (((x + dx) % XS) * YS + (y + dy) % YS) * 2 + core

    def source(peer):
        dx, dy = peer
        return (((x + dx) % XS) * YS + (y + YS - dy) % YS) * 2 + core

    barrier = pltpu.get_barrier_semaphore()
    partners = [*(target(peer) for peer in reversed(PEERS.values())), sibling]
    for partner in partners:
        pl.semaphore_signal(barrier, inc=1, device_id={"pre": partner}, device_id_type=MESH)

    own = pltpu.make_async_copy(q_hbm, near.at[OWN], load_sem.at[0])
    own.start()
    depth = width // ROOT_PARTS
    loads = [
        pltpu.make_async_copy(
            root_hbm.at[pl.ds(i * depth, depth)], keys.at[pl.ds(i * depth, depth)], load_sem.at[2 + i]
        )
        for i in range(ROOT_PARTS)
    ]
    loads.append(pltpu.make_async_copy(suffix_hbm, suffix, load_sem.at[1]))
    for load in loads:
        load.start()
    own.wait()
    pl.semaphore_wait(barrier, len(partners))

    def remote(src, dst, send, recv, device):
        return pltpu.make_async_remote_copy(
            src_ref=src,
            dst_ref=dst,
            send_sem=send,
            recv_sem=recv,
            device_id={"pre": device},
            device_id_type=MESH,
        )

    asks = {
        i: remote(near.at[OWN], near.at[i], ask_send, ask_recv.at[i], target(peer))
        for i, peer in PEERS.items()
    }
    passes = [
        remote(near.at[i], far.at[i], fwd_send, fwd_recv, sibling) for i in range(CHIPS)
    ]

    def pass_on(i):
        asks[i].wait_recv()
        passes[i].start()

    for ask in asks.values():
        ask.start()
    passes[OWN].start()
    for load in loads:
        load.wait()

    def turn(i, carry):
        at = pl.multiple_of(i * 512, 512)
        for k in range(4):
            values[pl.ds(at + k * 128, 128), :] = keys[:LATENT, pl.ds(at + k * 128, 128)].T
        return carry

    lax.fori_loop(0, positions // 512, turn, 0)
    for r in range(reqs):
        branch_values[r] = suffix[picks[r], :LATENT].T

    place = me * tail + lax.broadcasted_iota(jnp.int32, (1, tail), 1)

    calls = []

    def lane_sums(weight):
        return sum(weight[:, k * 128 : (k + 1) * 128] for k in range(weight.shape[1] // 128))

    def by_request(part):
        chips = part.shape[0]
        part = part.astype(jnp.float32)
        return [
            part[:, r * heads : (r + 1) * heads].reshape(chips * heads, part.shape[2])
            for r in range(reqs)
        ]

    def by_row(parts):
        parts = [part.reshape(-1, 1, heads, part.shape[1]) for part in parts]
        return jnp.concatenate(parts, axis=1).reshape(-1, parts[0].shape[3])

    def weigh(part, state):
        top = jnp.max(part, axis=1, keepdims=True)
        scale = None
        if state is not None:
            top = jnp.maximum(state[0], top)
            scale = jnp.exp2((state[0] - top) * EXP2_SCALE)
        return top, jnp.exp2((part - top) * EXP2_SCALE), scale

    def grown(state, top, weight, scale, out):
        sums = lane_sums(weight)
        if state is not None:
            sums, out = sums + state[1] * scale, out + state[2] * scale
        return top, sums, out

    def suffix_scores(asked):
        parts = []
        for r, mine in enumerate(by_request(asked)):
            part = jnp.dot(
                mine.astype(jnp.bfloat16), suffix[picks[r]], preferred_element_type=jnp.float32
            )
            parts.append(jnp.where(place < lengths[picks[r]], part, -jnp.inf))
        return by_row(parts)

    def suffix_products(weight):
        weight = weight.reshape(-1, rows, tail)
        return by_row(
            [
                jnp.dot(
                    mine.astype(jnp.bfloat16), branch_values[r], preferred_element_type=jnp.float32
                )
                for r, mine in enumerate(by_request(weight))
            ]
        )

    def attend(asked, state, between, both=None, other=None):
        query = asked.reshape(half, width)

        def score(j):
            return jnp.dot(
                query, keys[:, j * BLOCK : (j + 1) * BLOCK], preferred_element_type=jnp.float32
            )

        count = positions // BLOCK
        part = score(0)
        for j in range(count):
            following = score(j + 1) if j + 1 < count else None
            if both is not None and j == SUFFIX_AT:
                ends = suffix_scores(both)
            top, weight, scale = weigh(part, state)
            out = jnp.dot(
                weight.astype(jnp.bfloat16),
                values[j * BLOCK : (j + 1) * BLOCK, :],
                preferred_element_type=jnp.float32,
            )
            state, part = grown(state, top, weight, scale, out), following
            if both is not None and j == SUFFIX_AT:
                first, second = weigh(ends[:half], other), weigh(ends[half:], state)
                out = suffix_products(jnp.concatenate([first[1], second[1]]))
                other = grown(other, *first, out[:half])
                state = grown(state, *second, out[half:])
            for step in between.get(j, ()):
                step()
        return state if both is None else (other, state)

    row = lax.broadcasted_iota(jnp.int32, (rows, 128), 0)
    lane = lax.broadcasted_iota(jnp.int32, (rows, 128), 1)
    kept = []

    def store(near_rows, k, state):
        joint, sums, out = state
        base = (0 if near_rows else CHIPS) + k * HALF
        part_out[base : base + HALF] = out.astype(jnp.bfloat16).reshape(HALF, rows, LATENT)
        total = jnp.sum(sums, axis=1, keepdims=True)
        for j in range(HALF):
            part = slice(j * rows, (j + 1) * rows)
            stat = jnp.where(lane == row, joint[part], 0.0)
            stat = stat + jnp.where(lane == row + rows, total[part], 0.0)
            part_stat[base + j] = jnp.sum(stat, axis=0, keepdims=True)

    def send(near_rows, k):
        for slot in reversed(range(k * HALF, (k + 1) * HALF)):
            at = slot if near_rows else CHIPS + slot
            if near_rows and slot == OWN:
                pair = [
                    pltpu.make_async_copy(part_out.at[at], all_out.at[at], load_sem.at[0]),
                    pltpu.make_async_copy(part_stat.at[at], all_stat.at[at], load_sem.at[1]),
                ]
                kept.extend(pair)
            else:
                device = me if slot == OWN else source(PEERS[slot])
                device = device if near_rows else other_core(device)
                pair = [
                    remote(part_out.at[at], all_out.at[at], out_send, out_recv, device),
                    remote(part_stat.at[at], all_stat.at[at], stat_send, stat_recv, device),
                ]
            for copy in pair:
                copy.start()

    def hook(*slots):
        return [functools.partial(pass_on, i) for i in slots]

    for i in NEXT:
        pass_on(i)
    first = attend(near[:HALF], None, {0: hook(*SECOND)})
    for i in THIRD:
        pass_on(i)
    first, second = attend(near[HALF:], None, {}, near[...], first)
    store(True, 1, second)
    store(True, 0, first)
    send(True, 1)
    send(True, 0)
    every_pass = remote(near, far, fwd_send, fwd_recv, sibling)
    every_pass.wait_recv()
    first = (
        jnp.full((half, 1), FLOOR, jnp.float32),
        jnp.zeros((half, 128), jnp.float32),
        jnp.zeros((half, LATENT), jnp.float32),
    )
    first, second = attend(far[HALF:], None, {}, far[...], first)
    store(False, 1, second)
    send(False, 1)
    store(False, 0, attend(far[:HALF], first, {}))
    send(False, 0)
    most = pl.ds(0, 2 * CHIPS - 1)
    outs = remote(part_out.at[most], all_out.at[most], out_send, out_recv, sibling)
    stats = remote(part_stat.at[most], all_stat.at[most], stat_send, stat_recv, sibling)
    others = pl.ds(0, len(PEERS))
    every_ask = remote(near.at[others], near.at[others], ask_send, ask_recv.at[OWN], sibling)
    for copy in (every_ask, every_pass, outs, stats):
        copy.wait_send()
    for copy in kept:
        copy.wait()
    outs.wait_recv()
    stats.wait_recv()


def combine(all_out, all_stat, o_ref):
    rows = o_ref.shape[0]
    row = lax.broadcasted_iota(jnp.int32, (rows, 128), 0)
    lane = lax.broadcasted_iota(jnp.int32, (rows, 128), 1)
    stat = all_stat[...].reshape(2 * CHIPS, 128)
    high = jnp.max(stat, axis=0, keepdims=True)
    share = jnp.exp2((stat - high) * EXP2_SCALE)
    totals = pltpu.roll(stat, 128 - rows, 1)
    share = share / jnp.sum(share * totals, axis=0, keepdims=True)
    result = jnp.zeros((rows, LATENT), jnp.float32)
    for j in range(2 * CHIPS):
        column = jnp.sum(jnp.where(lane == row, share[j : j + 1], 0.0), axis=1, keepdims=True)
        result = result + all_out[j].astype(jnp.float32) * column
    o_ref[...] = result.astype(jnp.bfloat16)


def local(queries, root_latent, suffix_latent, suffix_length, branch_pick):
    reqs, heads, width = queries.shape
    rows = reqs * heads
    positions = root_latent.shape[0]
    tail = suffix_latent.shape[1]
    dma = pltpu.SemaphoreType.DMA
    parts = pl.pallas_call(
        kernel,
        out_shape=[
            jax.ShapeDtypeStruct((2 * CHIPS, rows, LATENT), jnp.bfloat16),
            jax.ShapeDtypeStruct((2 * CHIPS, 1, 128), jnp.float32),
        ],
        in_specs=[pl.BlockSpec(memory_space=pl.ANY)] * 3
        + [pl.BlockSpec(memory_space=pltpu.SMEM)] * 2,
        out_specs=[pl.BlockSpec(memory_space=pl.ANY)] * 2,
        scratch_shapes=[
            pltpu.VMEM((width, positions), jnp.bfloat16),
            pltpu.VMEM((positions, LATENT), jnp.bfloat16),
            pltpu.VMEM((reqs, width, tail), jnp.bfloat16),
            pltpu.VMEM((reqs, tail, LATENT), jnp.bfloat16),
            pltpu.VMEM((CHIPS, rows, width), jnp.bfloat16),
            pltpu.VMEM((CHIPS, rows, width), jnp.bfloat16),
            pltpu.VMEM((2 * CHIPS, rows, LATENT), jnp.bfloat16),
            pltpu.VMEM((2 * CHIPS, 1, 128), jnp.float32),
            dma((2 + ROOT_PARTS,)),
            dma,
            dma((CHIPS,)),
            dma,
            dma,
            dma,
            dma,
            dma,
            dma,
        ],
        compiler_params=pltpu.CompilerParams(
            collective_id=0, has_side_effects=True, vmem_limit_bytes=56 * 2**20
        ),
    )(
        queries.reshape(rows, width),
        root_latent.T,
        suffix_latent.transpose(0, 2, 1),
        suffix_length,
        branch_pick,
    )
    out = pl.pallas_call(
        combine,
        out_shape=jax.ShapeDtypeStruct((rows, LATENT), jnp.bfloat16),
        in_specs=[pl.BlockSpec(memory_space=pltpu.VMEM)] * 2,
        out_specs=pl.BlockSpec(memory_space=pltpu.VMEM),
    )(*parts)
    return out.reshape(reqs, heads, LATENT)


def solution(mesh):
    return jax.shard_map(
        local,
        mesh=mesh,
        in_specs=(P("req", "pre", None), P("pre", None), P("req", "pre", None), P("req"), P("req")),
        out_specs=P("req", "pre", None),
        check_vma=False,
    )
```

```python
import functools

import jax
import jax.numpy as jnp
from jax import lax
from jax.experimental import pallas as pl
from jax.experimental.pallas import tpu as pltpu
from jax.sharding import PartitionSpec as P

MESH = pl.DeviceIdType.MESH
LATENT = 512
SCORE_SCALE = 192.0 ** (-0.5)
EXP2_SCALE = SCORE_SCALE * 1.4426950408889634
YS, XS = 4, 2
CHIPS = XS * YS
PEERS = {0: (1, 0), 1: (0, 1), 2: (0, 3), 4: (1, 1), 5: (1, 3), 6: (0, 2), 7: (1, 2)}
OWN = 3
NEXT, SECOND, THIRD = (0, 1, 2), (4, 5), (6, 7)
HALF = CHIPS // 2
BLOCK = 2048
SUFFIX_AT = 1
FLOOR = -1e30
ROOT_PARTS = 4


def kernel(
    q_hbm,
    root_hbm,
    suffix_hbm,
    lengths_hbm,
    picks_hbm,
    all_out,
    all_stat,
    lengths,
    picks,
    keys,
    values,
    suffix,
    branch_values,
    near,
    far,
    part_out,
    part_stat,
    load_sem,
    ask_send,
    ask_recv,
    fwd_send,
    fwd_recv,
    out_send,
    out_recv,
    stat_send,
    stat_recv,
):
    me = lax.axis_index("pre")
    core = me % 2
    chip = me // 2
    x, y = chip // YS, chip % YS

    def other_core(device):
        return device + 1 - 2 * core

    sibling = other_core(me)
    reqs = lengths.shape[0]
    rows, width = q_hbm.shape
    heads = rows // reqs
    half = HALF * rows
    positions = root_hbm.shape[1]
    tail = suffix_hbm.shape[2]

    def target(peer):
        dx, dy = peer
        return (((x + dx) % XS) * YS + (y + dy) % YS) * 2 + core

    def source(peer):
        dx, dy = peer
        return (((x + dx) % XS) * YS + (y + YS - dy) % YS) * 2 + core

    barrier = pltpu.get_barrier_semaphore()
    partners = [*(target(peer) for peer in reversed(PEERS.values())), sibling]
    for partner in partners:
        pl.semaphore_signal(barrier, inc=1, device_id={"pre": partner}, device_id_type=MESH)

    own = pltpu.make_async_copy(q_hbm, near.at[OWN], load_sem.at[0])
    own.start()
    depth = width // ROOT_PARTS
    loads = [
        pltpu.make_async_copy(
            root_hbm.at[pl.ds(i * depth, depth)], keys.at[pl.ds(i * depth, depth)], load_sem.at[2 + i]
        )
        for i in range(ROOT_PARTS)
    ]
    loads += [
        pltpu.make_async_copy(suffix_hbm, suffix, load_sem.at[1]),
        pltpu.make_async_copy(lengths_hbm, lengths, load_sem.at[2 + ROOT_PARTS]),
        pltpu.make_async_copy(picks_hbm, picks, load_sem.at[3 + ROOT_PARTS]),
    ]
    for load in loads:
        load.start()
    own.wait()
    pl.semaphore_wait(barrier, len(partners))

    def remote(src, dst, send, recv, device):
        return pltpu.make_async_remote_copy(
            src_ref=src,
            dst_ref=dst,
            send_sem=send,
            recv_sem=recv,
            device_id={"pre": device},
            device_id_type=MESH,
        )

    asks = {
        i: remote(near.at[OWN], near.at[i], ask_send, ask_recv.at[i], target(peer))
        for i, peer in PEERS.items()
    }
    passes = [
        remote(near.at[i], far.at[i], fwd_send, fwd_recv, sibling) for i in range(CHIPS)
    ]

    def pass_on(i):
        asks[i].wait_recv()
        passes[i].start()

    for ask in asks.values():
        ask.start()
    passes[OWN].start()
    for load in loads:
        load.wait()

    def turn(at):
        values[pl.ds(at, 128), :] = keys[:LATENT, pl.ds(at, 128)].T

    def turn_some(i, carry):
        for k in range(4):
            turn(pl.multiple_of(i * 512 + k * 128, 128))
        return carry

    def turn_rest():
        for at in range(BLOCK, positions, 128):
            turn(at)
        for r in range(reqs):
            branch_values[r] = suffix[picks[r], :LATENT].T

    lax.fori_loop(0, BLOCK // 512, turn_some, 0)

    place = me * tail + lax.broadcasted_iota(jnp.int32, (1, tail), 1)

    calls = []

    def lane_sums(weight):
        return sum(weight[:, k * 128 : (k + 1) * 128] for k in range(weight.shape[1] // 128))

    def by_request(part):
        chips = part.shape[0]
        part = part.astype(jnp.float32)
        return [
            part[:, r * heads : (r + 1) * heads].reshape(chips * heads, part.shape[2])
            for r in range(reqs)
        ]

    def by_row(parts):
        parts = [part.reshape(-1, 1, heads, part.shape[1]) for part in parts]
        return jnp.concatenate(parts, axis=1).reshape(-1, parts[0].shape[3])

    def weigh(part, state):
        top = jnp.max(part, axis=1, keepdims=True)
        scale = None
        if state is not None:
            top = jnp.maximum(state[0], top)
            scale = jnp.exp2((state[0] - top) * EXP2_SCALE)
        return top, jnp.exp2((part - top) * EXP2_SCALE), scale

    def grown(state, top, weight, scale, out):
        sums = lane_sums(weight)
        if state is not None:
            sums, out = sums + state[1] * scale, out + state[2] * scale
        return top, sums, out

    def suffix_scores(asked):
        parts = []
        for r, mine in enumerate(by_request(asked)):
            part = jnp.dot(
                mine.astype(jnp.bfloat16), suffix[picks[r]], preferred_element_type=jnp.float32
            )
            parts.append(jnp.where(place < lengths[picks[r]], part, -jnp.inf))
        return by_row(parts)

    def suffix_products(weight):
        weight = weight.reshape(-1, rows, tail)
        return by_row(
            [
                jnp.dot(
                    mine.astype(jnp.bfloat16), branch_values[r], preferred_element_type=jnp.float32
                )
                for r, mine in enumerate(by_request(weight))
            ]
        )

    def attend(asked, state, between, both=None, other=None):
        query = asked.reshape(half, width)

        def score(j):
            here = slice(j * BLOCK, (j + 1) * BLOCK)
            return jnp.dot(
                query[:, :LATENT], keys[:LATENT, here], preferred_element_type=jnp.float32
            ) + jnp.dot(query[:, LATENT:], keys[LATENT:, here], preferred_element_type=jnp.float32)

        count = positions // BLOCK
        part = score(0)
        for j in range(count):
            following = score(j + 1) if j + 1 < count else None
            if both is not None and j == SUFFIX_AT:
                ends = suffix_scores(both)
            top, weight, scale = weigh(part, state)
            out = jnp.dot(
                weight.astype(jnp.bfloat16),
                values[j * BLOCK : (j + 1) * BLOCK, :],
                preferred_element_type=jnp.float32,
            )
            state, part = grown(state, top, weight, scale, out), following
            if both is not None and j == SUFFIX_AT:
                first, second = weigh(ends[:half], other), weigh(ends[half:], state)
                out = suffix_products(jnp.concatenate([first[1], second[1]]))
                other = grown(other, *first, out[:half])
                state = grown(state, *second, out[half:])
            for step in between.get(j, ()):
                step()
        return state if both is None else (other, state)

    row = lax.broadcasted_iota(jnp.int32, (rows, 128), 0)
    lane = lax.broadcasted_iota(jnp.int32, (rows, 128), 1)
    kept = []

    def store(near_rows, k, state):
        joint, sums, out = state
        base = (0 if near_rows else CHIPS) + k * HALF
        part_out[base : base + HALF] = out.astype(jnp.bfloat16).reshape(HALF, rows, LATENT)
        total = jnp.sum(sums, axis=1, keepdims=True)
        for j in range(HALF):
            part = slice(j * rows, (j + 1) * rows)
            stat = jnp.where(lane == row, joint[part], 0.0)
            stat = stat + jnp.where(lane == row + rows, total[part], 0.0)
            part_stat[base + j] = jnp.sum(stat, axis=0, keepdims=True)

    def send(near_rows, k):
        for slot in reversed(range(k * HALF, (k + 1) * HALF)):
            at = slot if near_rows else CHIPS + slot
            if near_rows and slot == OWN:
                pair = [
                    pltpu.make_async_copy(part_out.at[at], all_out.at[at], load_sem.at[0]),
                    pltpu.make_async_copy(part_stat.at[at], all_stat.at[at], load_sem.at[1]),
                ]
                kept.extend(pair)
            else:
                device = me if slot == OWN else source(PEERS[slot])
                device = device if near_rows else other_core(device)
                pair = [
                    remote(part_out.at[at], all_out.at[at], out_send, out_recv, device),
                    remote(part_stat.at[at], all_stat.at[at], stat_send, stat_recv, device),
                ]
            for copy in pair:
                copy.start()

    def hook(*slots):
        return [functools.partial(pass_on, i) for i in slots]

    for i in NEXT:
        pass_on(i)
    first = attend(near[:HALF], None, {0: [turn_rest, *hook(*SECOND)]})
    for i in THIRD:
        pass_on(i)
    first, second = attend(near[HALF:], None, {}, near[...], first)
    store(True, 1, second)
    store(True, 0, first)
    send(True, 1)
    send(True, 0)
    every_pass = remote(near, far, fwd_send, fwd_recv, sibling)
    every_pass.wait_recv()
    first = (
        jnp.full((half, 1), FLOOR, jnp.float32),
        jnp.zeros((half, 128), jnp.float32),
        jnp.zeros((half, LATENT), jnp.float32),
    )
    first, second = attend(far[HALF:], None, {}, far[...], first)
    store(False, 1, second)
    send(False, 1)
    store(False, 0, attend(far[:HALF], first, {}))
    send(False, 0)
    most = pl.ds(0, 2 * CHIPS - 1)
    outs = remote(part_out.at[most], all_out.at[most], out_send, out_recv, sibling)
    stats = remote(part_stat.at[most], all_stat.at[most], stat_send, stat_recv, sibling)
    others = pl.ds(0, len(PEERS))
    every_ask = remote(near.at[others], near.at[others], ask_send, ask_recv.at[OWN], sibling)
    for copy in (every_ask, every_pass, outs, stats):
        copy.wait_send()
    for copy in kept:
        copy.wait()
    outs.wait_recv()
    stats.wait_recv()


def combine(all_out, all_stat, o_ref):
    rows = o_ref.shape[0]
    row = lax.broadcasted_iota(jnp.int32, (rows, 128), 0)
    lane = lax.broadcasted_iota(jnp.int32, (rows, 128), 1)
    stat = all_stat[...].reshape(2 * CHIPS, 128)
    high = jnp.max(stat, axis=0, keepdims=True)
    share = jnp.exp2((stat - high) * EXP2_SCALE)
    totals = pltpu.roll(stat, 128 - rows, 1)
    share = share / jnp.sum(share * totals, axis=0, keepdims=True)
    result = jnp.zeros((rows, LATENT), jnp.float32)
    for j in range(2 * CHIPS):
        column = jnp.sum(jnp.where(lane == row, share[j : j + 1], 0.0), axis=1, keepdims=True)
        result = result + all_out[j].astype(jnp.float32) * column
    o_ref[...] = result.astype(jnp.bfloat16)


def local(queries, root_latent, suffix_latent, suffix_length, branch_pick):
    reqs, heads, width = queries.shape
    rows = reqs * heads
    positions = root_latent.shape[0]
    tail = suffix_latent.shape[1]
    dma = pltpu.SemaphoreType.DMA
    parts = pl.pallas_call(
        kernel,
        out_shape=[
            jax.ShapeDtypeStruct((2 * CHIPS, rows, LATENT), jnp.bfloat16),
            jax.ShapeDtypeStruct((2 * CHIPS, 1, 128), jnp.float32),
        ],
        in_specs=[pl.BlockSpec(memory_space=pl.ANY)] * 5,
        out_specs=[pl.BlockSpec(memory_space=pl.ANY)] * 2,
        scratch_shapes=[
            pltpu.SMEM((reqs,), jnp.int32),
            pltpu.SMEM((reqs,), jnp.int32),
            pltpu.VMEM((width, positions), jnp.bfloat16),
            pltpu.VMEM((positions, LATENT), jnp.bfloat16),
            pltpu.VMEM((reqs, width, tail), jnp.bfloat16),
            pltpu.VMEM((reqs, tail, LATENT), jnp.bfloat16),
            pltpu.VMEM((CHIPS, rows, width), jnp.bfloat16),
            pltpu.VMEM((CHIPS, rows, width), jnp.bfloat16),
            pltpu.VMEM((2 * CHIPS, rows, LATENT), jnp.bfloat16),
            pltpu.VMEM((2 * CHIPS, 1, 128), jnp.float32),
            dma((4 + ROOT_PARTS,)),
            dma,
            dma((CHIPS,)),
            dma,
            dma,
            dma,
            dma,
            dma,
            dma,
        ],
        compiler_params=pltpu.CompilerParams(
            collective_id=0, has_side_effects=True, vmem_limit_bytes=56 * 2**20
        ),
    )(
        queries.reshape(rows, width),
        root_latent.T,
        suffix_latent.transpose(0, 2, 1),
        suffix_length,
        branch_pick,
    )
    out = pl.pallas_call(
        combine,
        out_shape=jax.ShapeDtypeStruct((rows, LATENT), jnp.bfloat16),
        in_specs=[pl.BlockSpec(memory_space=pltpu.VMEM)] * 2,
        out_specs=pl.BlockSpec(memory_space=pltpu.VMEM),
    )(*parts)
    return out.reshape(reqs, heads, LATENT)


def solution(mesh):
    return jax.shard_map(
        local,
        mesh=mesh,
        in_specs=(P("req", "pre", None), P("pre", None), P("req", "pre", None), P("req"), P("req")),
        out_specs=P("req", "pre", None),
        check_vma=False,
    )
```
